128 devices in a mesh: rep: 16 (over z, x_hi, core), fsdp: 8 (over y, x_lo).
Axes of the slice: x: 4 (x_hi: 2, x_lo: 2; x = x_hi * 2 + x_lo), y: 4, z: 4, core: 2. Of those that a mesh axis runs over, the one named last changes fastest.
Arguments:
- tokens: bfloat16 [16, 2, 1024, 8192], P('rep', None, 'fsdp'), may hold values from -6 to 6
- targets: bfloat16 [16, 2, 1024, 1024], P('rep', None, 'fsdp'), may hold values from -6 to 6
- params: float32 [16, 8192, 1024], P('rep', 'fsdp'), may hold values from -6 to 6
- moment1: bfloat16 [16, 8192, 1024], P('rep', 'fsdp'), may hold values from -2 to 2
- moment2: bfloat16 [16, 8192, 1024], P('rep', 'fsdp'), may hold values from 0.0099487305 to 1
- stale_delta: float32 [16, 8192, 512], P('rep', 'fsdp'), may hold values from -6 to 6
- anchor: float32 [2, 8, 1024, 512], P(None, 'fsdp', 'rep'), may hold values from -6 to 6
- momentum: float32 [2, 8, 1024, 512], P(None, 'fsdp', 'rep'), may hold values from -4 to 4
- plan: int32 [1], replicated, may hold values from 0 to 1
Outputs:
- params_out: float32 [16, 8192, 1024], P('rep', 'fsdp')
- moment1_out: bfloat16 [16, 8192, 1024], P('rep', 'fsdp')
- moment2_out: bfloat16 [16, 8192, 1024], P('rep', 'fsdp')
- anchor_out: float32 [2, 8, 1024, 512], P(None, 'fsdp', 'rep')
- momentum_out: float32 [2, 8, 1024, 512], P(None, 'fsdp', 'rep')
The draws below stay inside these ranges and needn't reach their ends.
All inputs are finite; a program needn't handle non-finite values.
Results may differ from the reference program's by a relative error of at most 0.011.
Values may be sent and summed in bfloat16 or wider, within the bound.
No kernel may reach another device: no remote copies, remote signals or barrier semaphores. Data moves between devices by JAX's collectives and lax.ppermute only.
A program may use at most 128 MiB of HBM per device.

```python
import math
import jax
import jax.numpy as jnp
from jax import lax

D = 8192
KV = 1024
FRAGS = 2
STEPS = 2
FRAG_W = 512
REPS = 16
TOK_REP = 1024
ROWS_F = 1024
N_REP = 16
N_FSDP = 8


def spiked(drawn, stream_key, source, target, parts, factor):
    owner, partner = [(jnp.arange(drawn.shape[position]) // (drawn.shape[position] // parts)).reshape([-1 if axis == position else 1 for axis in range(drawn.ndim)]) for position in (source, target)]
    chosen = jax.random.permutation(stream_key, parts)[partner]
    strong = (owner == chosen) | (owner == (partner + parts // 2) % parts)
    return jnp.where(strong, factor * drawn, drawn)


def block_scale(own_key, extent, split, smallest, high):
    level, own = 1.0, jax.random.fold_in(own_key, 6)
    for axis_at, parts in split:
        draws = jnp.exp(jax.random.uniform(jax.random.fold_in(own, axis_at), (parts,), jnp.float32, smallest / len(split), high / len(split)))
        level = level * jnp.repeat(draws, extent[axis_at] // parts).reshape([-1 if axis == axis_at else 1 for axis in range(len(extent))])
    return level


def bell_draw(key, shape, deviation, limit, cuts=(), kind=jnp.bfloat16):
    array = jax.random.normal(key, shape, jnp.float32) * deviation
    if len(cuts) > 0:
        array = block_scale(key, shape, cuts, -0.22, 0.18) * array
    return jnp.clip(array, min=-limit, max=limit).astype(kind)


def bell_draw_with(key, dims, width, reach, split, heavy, kind=jnp.bfloat16):
    drawn = width * jax.random.normal(key, dims, jnp.float32)
    if split:
        drawn = drawn * block_scale(key, dims, split, -0.22, 0.18)
    return jnp.clip(spiked(drawn, jax.random.fold_in(key, 3), *heavy), -reach, reach).astype(kind)


def setup_inputs(seed: int = 0) -> dict:
    key_list = jax.random.split(jax.random.key(seed), 10)
    tokens = bell_draw(key_list[0], (REPS, STEPS, TOK_REP, D), 1.0, 6.0, ((0, 16), (2, 8)))
    targets = bell_draw(key_list[1], (REPS, STEPS, TOK_REP, KV), 1.0, 6.0, ((0, 16), (2, 8)))
    params = bell_draw(key_list[2], (REPS, D, KV), 1.0, 6.0, ((0, 16), (1, 8)), jnp.float32)
    moment1 = bell_draw(key_list[3], (REPS, D, KV), 0.3, 2.0, ((0, 16), (1, 8)))
    moment2 = jnp.clip(jnp.exp(math.log(1.0) - 4.61031033 * jax.random.uniform(key_list[4], (REPS, D, KV), jnp.float32) ** block_scale(key_list[4], (REPS, D, KV), ((0, 16), (1, 8)), -0.2, 0.2)), 0.0099487305, 1.0).astype(jnp.bfloat16)
    stale_delta = bell_draw_with(key_list[5], (REPS, D, FRAG_W), 1.0, 6.0, ((0, 16), (1, 8)), (0, 1, 16, 2.0), jnp.float32)
    anchor = bell_draw(key_list[6], (FRAGS, N_FSDP, ROWS_F, FRAG_W), 1.0, 6.0, ((1, 8), (2, 16)), jnp.float32)
    momentum = bell_draw(key_list[7], (FRAGS, N_FSDP, ROWS_F, FRAG_W), 0.5, 4.0, ((1, 8), (2, 16)), jnp.float32)
    plan = jax.random.randint(key_list[8], (1,), 0, FRAGS).astype(jnp.int32)
    return {"tokens": tokens, "targets": targets, "params": params, "moment1": moment1, "moment2": moment2, "stale_delta": stale_delta, "anchor": anchor, "momentum": momentum, "plan": plan}


beta_one = 0.9
beta_two = 0.95
inner_rate = 0.02
decay_rate = 0.1
adam_eps = 1e-08
outer_rate = 0.7
outer_mu = 0.9
mix_weight = 0.5

def stored(value):
    return lax.optimization_barrier(value.astype(jnp.bfloat16))

def replica_window(items):
    weights, first_b, second_b, tok_steps, tgt_steps = items
    inv_root = 1.0 / math.sqrt(D)
    first = first_b.astype(jnp.float32)
    second = second_b.astype(jnp.float32)
    for step in range(STEPS):
        narrow = weights.astype(jnp.bfloat16)
        keys = jnp.dot(tok_steps[step], narrow, preferred_element_type=jnp.float32) * inv_root
        resid = (keys - tgt_steps[step].astype(jnp.float32)).astype(jnp.bfloat16)
        grad = lax.dot_general(tok_steps[step], resid, (((0,), (0,)), ((), ())), preferred_element_type=jnp.float32) * inv_root
        first = beta_one * first + (1.0 - beta_one) * grad
        second = beta_two * second + (1.0 - beta_two) * grad * grad
        weights = weights - inner_rate * (first / (jnp.sqrt(second) + adam_eps) + decay_rate * weights)
        first_b = stored(first)
        second_b = stored(second)
        first = first_b.astype(jnp.float32)
        second = second_b.astype(jnp.float32)
    return (weights, first_b, second_b)

def reference(tokens, targets, params, moment1, moment2, stale_delta, anchor, momentum, plan):
    weights, first_b, second_b = lax.map(replica_window, (params, moment1, moment2, tokens, targets))
    fragment = plan[0]
    mean_delta = lax.optimization_barrier(jnp.sum(stale_delta, axis=0)) / N_REP
    anchor_frag = lax.dynamic_index_in_dim(anchor, fragment, 0, keepdims=False).reshape(D, FRAG_W)
    moment_frag = lax.dynamic_index_in_dim(momentum, fragment, 0, keepdims=False).reshape(D, FRAG_W)
    moment_new = outer_mu * moment_frag + mean_delta
    anchor_new = anchor_frag - outer_rate * (mean_delta + outer_mu * moment_new)
    anchor_out = lax.dynamic_update_index_in_dim(anchor, anchor_new.reshape(N_FSDP, D // N_FSDP, FRAG_W), fragment, 0)
    momentum_out = lax.dynamic_update_index_in_dim(momentum, moment_new.reshape(N_FSDP, D // N_FSDP, FRAG_W), fragment, 0)
    column = fragment * FRAG_W
    local_cols = lax.dynamic_slice_in_dim(weights, column, FRAG_W, 2)
    mixed = mix_weight * local_cols + (1.0 - mix_weight) * anchor_new[None]
    weights = lax.dynamic_update_slice_in_dim(weights, mixed, column, 2)
    return (weights, first_b, second_b, anchor_out, momentum_out)
```

```python
import math

import jax
import jax.numpy as jnp
from jax import lax
from jax.experimental import pallas as pl
from jax.experimental.pallas import tpu as pltpu
from jax.sharding import PartitionSpec as P

beta_one = 0.9
beta_two = 0.95
inner_rate = 0.02
decay_rate = 0.1
adam_eps = 1e-08
outer_rate = 0.7
outer_mu = 0.9
mix_weight = 0.5

f32 = jnp.float32
bf16 = jnp.bfloat16
VMEM_LIMIT = 48 * 1024 * 1024

N_Y = 4
N_X = 2


def swap_x(value):
    return lax.ppermute(value, "fsdp", [(i, i ^ 1) for i in range(N_Y * N_X)])


def shift_y(value, hops):
    size = N_Y * N_X
    return lax.ppermute(value, "fsdp", [(i, (i + N_X * hops) % size) for i in range(size)])


def regroup_tokens(tokens, step):
    _, _, rows, width = tokens.shape
    parts = N_Y * N_X
    cols = width // parts

    def body(src, dst, sems):
        copies = [
            pltpu.make_async_copy(
                src.at[0, step, :, pl.ds(part * cols, cols)], dst.at[part], sems.at[part]
            )
            for part in range(parts)
        ]
        for copy in copies:
            copy.start()
        for copy in copies:
            copy.wait()

    return pl.pallas_call(
        body,
        out_shape=jax.ShapeDtypeStruct((parts, rows, cols), tokens.dtype),
        in_specs=[pl.BlockSpec(memory_space=pl.ANY)],
        out_specs=pl.BlockSpec(memory_space=pl.ANY),
        scratch_shapes=[pltpu.SemaphoreType.DMA((parts,))],
        cost_estimate=pl.CostEstimate(flops=0, bytes_accessed=4 * rows * width, transcendentals=0),
        name="regroup_tokens",
    )(tokens)


def pair_rows(y_pos, hops, pair):
    return pl.multiple_of(lax.rem(y_pos + hops, N_Y) * pair, pair)


def first_keys(y_pos, toks, weights, chain, cols):
    rows, width = toks.shape
    pair = rows // N_Y

    def body(y_ref, tok_ref, w_ref, own_ref, *out_refs):
        narrow = w_ref[0].astype(bf16)
        for hops in (1, 2, 3, 0):
            at = pair_rows(y_ref[0], hops, pair)
            part = jnp.dot(tok_ref[pl.ds(at, pair), :], narrow, preferred_element_type=f32)
            if hops:
                out_refs[hops - 1][...] = part.astype(bf16)
            else:
                own_ref[...] = part

    whole = lambda i, y: (0, 0)
    return pl.pallas_call(
        body,
        grid_spec=pltpu.PrefetchScalarGridSpec(
            num_scalar_prefetch=1,
            grid=(1,),
            in_specs=[
                pl.BlockSpec((rows, width), whole),
                pl.BlockSpec((1, width, cols), lambda i, y: (0, 0, chain)),
            ],
            out_specs=[pl.BlockSpec((pair, cols), whole)] * N_Y,
        ),
        out_shape=[jax.ShapeDtypeStruct((pair, cols), f32)]
        + [jax.ShapeDtypeStruct((pair, cols), bf16)] * (N_Y - 1),
        compiler_params=pltpu.CompilerParams(vmem_limit_bytes=VMEM_LIMIT),
        cost_estimate=pl.CostEstimate(
            flops=2 * rows * width * cols,
            bytes_accessed=2 * rows * width + 4 * width * cols + 2 * rows * cols,
            transcendentals=0,
        ),
        name="first_keys",
    )(y_pos, toks, weights)


def adam(grad, first, second, weights):
    first = beta_one * first.astype(f32) + (1.0 - beta_one) * grad
    second = beta_two * second.astype(f32) + (1.0 - beta_two) * grad * grad
    weights = weights - inner_rate * (
        first / (jnp.sqrt(second) + adam_eps) + decay_rate * weights
    )
    return first, second, weights


def gather_resid(y_ref, resid_refs, full, pair):
    for hops in range(N_Y):
        at = pair_rows(y_ref[0], (N_Y - hops) % N_Y, pair)
        full[pl.ds(at, pair), :] = resid_refs[hops][...]


def grad_block(tok, resid, inv_root):
    return (
        lax.dot_general(tok, resid, (((0,), (0,)), ((), ())), preferred_element_type=f32)
        * inv_root
    )


def middle_step(y_pos, toks, next_toks, resids, weights, first, second, chain, cols, inv_root):
    rows, width = toks.shape
    pair = rows // N_Y
    tile = 256
    tiles = width // tile

    def body(y_ref, tok_ref, next_ref, r0, r1, r2, r3, w_ref, m_ref, v_ref,
             w_out, m_out, v_out, own_ref, k1, k2, k3, full, narrow):
        step = pl.program_id(0)

        @pl.when(step == 0)
        def _():
            gather_resid(y_ref, (r0, r1, r2, r3), full, pair)

        grad = grad_block(tok_ref[...], full[...], inv_root)
        m_new, v_new, w_new = adam(grad, m_ref[0], v_ref[0], w_ref[0])
        w_out[...] = w_new
        m_out[...] = m_new.astype(bf16)
        v_out[...] = v_new.astype(bf16)
        narrow[pl.ds(pl.multiple_of(step * tile, tile), tile), :] = w_new.astype(bf16)

        @pl.when(step == tiles - 1)
        def _():
            for hops in (1, 2, 3, 0):
                at = pair_rows(y_ref[0], hops, pair)
                part = jnp.dot(
                    next_ref[pl.ds(at, pair), :], narrow[...], preferred_element_type=f32
                )
                if hops:
                    (k1, k2, k3)[hops - 1][...] = part.astype(bf16)
                else:
                    own_ref[...] = part

    whole = lambda i, y: (0, 0)
    state = lambda i, y: (0, i, chain)
    return pl.pallas_call(
        body,
        grid_spec=pltpu.PrefetchScalarGridSpec(
            num_scalar_prefetch=1,
            grid=(tiles,),
            in_specs=[
                pl.BlockSpec((rows, tile), lambda i, y: (0, i)),
                pl.BlockSpec((rows, width), whole),
            ]
            + [pl.BlockSpec((pair, cols), whole)] * N_Y
            + [pl.BlockSpec((1, tile, cols), state)] * 3,
            out_specs=[pl.BlockSpec((tile, cols), lambda i, y: (i, 0))] * 3
            + [pl.BlockSpec((pair, cols), whole)] * N_Y,
            scratch_shapes=[pltpu.VMEM((rows, cols), bf16), pltpu.VMEM((width, cols), bf16)],
        ),
        out_shape=[
            jax.ShapeDtypeStruct((width, cols), f32),
            jax.ShapeDtypeStruct((width, cols), bf16),
            jax.ShapeDtypeStruct((width, cols), bf16),
            jax.ShapeDtypeStruct((pair, cols), f32),
        ]
        + [jax.ShapeDtypeStruct((pair, cols), bf16)] * (N_Y - 1),
        compiler_params=pltpu.CompilerParams(vmem_limit_bytes=VMEM_LIMIT),
        cost_estimate=pl.CostEstimate(
            flops=4 * rows * width * cols,
            bytes_accessed=4 * rows * width + 18 * width * cols + 4 * rows * cols,
            transcendentals=width * cols,
        ),
        name="middle_step",
    )(y_pos, toks, next_toks, *resids, weights, first, second)


def last_step(y_pos, fragment, toks, resids, weights, first, second, anchor_new, chain, cols,
              inv_root, outs):
    rows, width = toks.shape
    pair = rows // N_Y
    tile = 256
    tiles = width // tile
    total = outs[0].shape[2] if outs is not None else 2 * cols

    def body(y_ref, f_ref, tok_ref, r0, r1, r2, r3, w_ref, m_ref, v_ref, a_ref, *rest):
        w_out, m_out, v_out, full = rest[-4:]

        @pl.when(pl.program_id(0) == 0)
        def _():
            gather_resid(y_ref, (r0, r1, r2, r3), full, pair)

        grad = grad_block(tok_ref[...], full[...], inv_root)
        m_new, v_new, w_new = adam(grad, m_ref[...], v_ref[...], w_ref[...])
        m_out[0] = m_new.astype(bf16)
        v_out[0] = v_new.astype(bf16)
        mixed = mix_weight * w_new + (1.0 - mix_weight) * a_ref[...].astype(f32)
        w_out[0] = jnp.where(f_ref[0] == chain, mixed, w_new)

    whole = lambda i, y, f: (0, 0)
    by_tile = lambda i, y, f: (i, 0)
    place = lambda i, y, f: (0, i, chain)
    in_specs = (
        [pl.BlockSpec((rows, tile), lambda i, y, f: (0, i))]
        + [pl.BlockSpec((pair, cols), whole)] * N_Y
        + [pl.BlockSpec((tile, cols), by_tile)] * 4
    )
    args = [y_pos, fragment, toks, *resids, weights, first, second, anchor_new]
    aliases = {}
    if outs is not None:
        in_specs = in_specs + [pl.BlockSpec(memory_space=pl.ANY)] * 3
        aliases = {len(args) + i: i for i in range(3)}
        args = args + list(outs)
    return pl.pallas_call(
        body,
        grid_spec=pltpu.PrefetchScalarGridSpec(
            num_scalar_prefetch=2,
            grid=(tiles,),
            in_specs=in_specs,
            out_specs=[pl.BlockSpec((1, tile, cols), place)] * 3,
            scratch_shapes=[pltpu.VMEM((rows, cols), bf16)],
        ),
        out_shape=[
            jax.ShapeDtypeStruct((1, width, total), f32),
            jax.ShapeDtypeStruct((1, width, total), bf16),
            jax.ShapeDtypeStruct((1, width, total), bf16),
        ],
        input_output_aliases=aliases,
        compiler_params=pltpu.CompilerParams(vmem_limit_bytes=VMEM_LIMIT),
        cost_estimate=pl.CostEstimate(
            flops=2 * rows * width * cols,
            bytes_accessed=2 * rows * width + 18 * width * cols + 2 * rows * cols,
            transcendentals=width * cols,
        ),
        name="last_step",
    )(*args)


def outer_step(shares, anchor, momentum, fragment, replicas):
    mean = jnp.sum(shares.astype(f32), axis=0) / replicas
    anchor_old = lax.dynamic_index_in_dim(anchor, fragment, 0, keepdims=False)[0]
    moment_old = lax.dynamic_index_in_dim(momentum, fragment, 0, keepdims=False)[0]
    moment_new = outer_mu * moment_old + mean
    anchor_new = anchor_old - outer_rate * (mean + outer_mu * moment_new)
    anchor_out = lax.dynamic_update_index_in_dim(anchor, anchor_new[None], fragment, 0)
    momentum_out = lax.dynamic_update_index_in_dim(momentum, moment_new[None], fragment, 0)
    return anchor_new, anchor_out, momentum_out


def on_device(tokens, targets, params, moment1, moment2, stale_delta, anchor, momentum, plan):
    inv_root = 1.0 / math.sqrt(tokens.shape[3])
    replicas = lax.axis_size("rep")
    place = lax.axis_index("fsdp")
    y_pos = jnp.full((1,), place // N_X, jnp.int32)
    x_pos = place % N_X
    cols = stale_delta.shape[2]
    chains = params.shape[2] // cols
    slice_rows = anchor.shape[2]

    def exchange(blocks, axis):
        return lax.all_to_all(blocks, axis, split_axis=0, concat_axis=0, tiled=True)

    flat = lambda blocks: blocks.reshape(-1, blocks.shape[-1])
    toks = [flat(exchange(regroup_tokens(tokens, step), "fsdp")) for step in range(2)]

    other = swap_x(targets[0])
    pair_targets = jnp.where(
        x_pos == 0,
        jnp.concatenate([targets[0], other], axis=1),
        jnp.concatenate([other, targets[0]], axis=1),
    )

    shares = exchange(
        stale_delta[0].astype(bf16).reshape(replicas, slice_rows, cols), "rep"
    )
    anchor_new, anchor_out, momentum_out = outer_step(shares, anchor, momentum, plan[0], replicas)
    spread = jnp.broadcast_to(anchor_new.astype(bf16)[None], (replicas, slice_rows, cols))
    anchor_full = flat(exchange(spread, "rep"))

    def resid_of(parts, step, chain):
        own, *sent = parts
        got = [shift_y(sent[hops - 1], hops) for hops in (1, 2, 3)]
        half = (own + got[0].astype(f32) + got[1].astype(f32) + got[2].astype(f32)).astype(bf16)
        keys = (half.astype(f32) + swap_x(half).astype(f32)) * inv_root
        goal = pair_targets[step, :, chain * cols : (chain + 1) * cols].astype(f32)
        resid = (keys - goal).astype(bf16)
        return [resid] + [shift_y(resid, hops) for hops in (1, 2, 3)]

    parts = [first_keys(y_pos, toks[0], params, chain, cols) for chain in range(chains)]
    state = []
    for chain in range(chains):
        resids = resid_of(parts[chain], 0, chain)
        w, m, v, *parts[chain] = middle_step(
            y_pos, toks[0], toks[1], resids, params, moment1, moment2, chain, cols, inv_root
        )
        state.append((w, m, v))
    outs = None
    for chain in range(chains):
        resids = resid_of(parts[chain], 1, chain)
        outs = last_step(
            y_pos, plan, toks[1], resids, *state[chain], anchor_full, chain, cols, inv_root, outs
        )
    return (*outs, anchor_out, momentum_out)


def solution(mesh):
    return jax.shard_map(
        on_device,
        mesh=mesh,
        in_specs=(
            P("rep", None, "fsdp", None),
            P("rep", None, "fsdp", None),
            P("rep", "fsdp", None),
            P("rep", "fsdp", None),
            P("rep", "fsdp", None),
            P("rep", "fsdp", None),
            P(None, "fsdp", "rep", None),
            P(None, "fsdp", "rep", None),
            P(),
        ),
        out_specs=(
            P("rep", "fsdp", None),
            P("rep", "fsdp", None),
            P("rep", "fsdp", None),
            P(None, "fsdp", "rep", None),
            P(None, "fsdp", "rep", None),
        ),
        check_vma=False,
    )
```

```python
import math

import jax
import jax.numpy as jnp
from jax import lax
from jax.experimental import pallas as pl
from jax.experimental.pallas import tpu as pltpu
from jax.sharding import PartitionSpec as P

beta_one = 0.9
beta_two = 0.95
inner_rate = 0.02
decay_rate = 0.1
adam_eps = 1e-08
outer_rate = 0.7
outer_mu = 0.9
mix_weight = 0.5

f32 = jnp.float32
bf16 = jnp.bfloat16

RING = 4
FSDP = 8
REP = 16
TILE = 256
ORDER = (('sides', 'A', 'B', 'outer', 'A', 'pairs', 'B', 'A', 'ring', 'B', 'join'), ('A', 'B', 'A', 'B'))
MODES = (
    (("up", "up"), ("down", "down")),
    (("direct", "direct"), ("direct", "direct")),
)


def swap_x(value):
    return lax.ppermute(value, "fsdp", [(i, i ^ 1) for i in range(FSDP)])


def shift_y(value, hops):
    return lax.ppermute(value, "fsdp", [(i, (i + 2 * hops) % FSDP) for i in range(FSDP)])


def swap_core(value):
    return lax.ppermute(value, "rep", [(i, i ^ 1) for i in range(REP)])


def swap_far(value):
    return lax.ppermute(value, "rep", [(i, i ^ 2) for i in range(REP)])


def shift_z(value, hops):
    return lax.ppermute(value, "rep", [(i, (i + 4 * hops) % REP) for i in range(REP)])


def in_vmem(value):
    return pltpu.with_memory_space_constraint(value, pltpu.VMEM)


def in_hbm(value):
    return pltpu.with_memory_space_constraint(value, pltpu.HBM)


def call(body, name, place, arrays, outs, scratch=(), limit=8, flops=0, apart=(), out_hbm=False,
         aliases=None):
    vmem = pl.BlockSpec(memory_space=pltpu.VMEM)
    hbm = pl.BlockSpec(memory_space=pl.ANY)
    out = pl.BlockSpec(memory_space=pltpu.HBM) if out_hbm else vmem
    moved = sum(math.prod(a.shape) * a.dtype.itemsize for a in list(arrays) + list(apart))
    moved += sum(math.prod(shape) * jnp.dtype(kind).itemsize for shape, kind in outs)
    return pl.pallas_call(
        body,
        in_specs=[pl.BlockSpec(memory_space=pltpu.SMEM)] * (place is not None)
        + [vmem] * len(arrays) + [hbm] * len(apart),
        out_specs=[out] * len(outs),
        out_shape=[
            (pltpu.HBM if out_hbm else pltpu.VMEM)(shape, kind)
            for shape, kind in outs
        ],
        scratch_shapes=list(scratch),
        input_output_aliases=aliases or {},
        compiler_params=pltpu.CompilerParams(vmem_limit_bytes=limit * 1024 * 1024),
        cost_estimate=pl.CostEstimate(flops=0, bytes_accessed=1024, transcendentals=0),
        name=name,
    )(*([] if place is None else [place]), *[in_vmem(array) for array in arrays], *apart)


def through_vmem(pairs, held, in_sems, out_sems):
    loads = [
        pltpu.make_async_copy(src, held.at[i], in_sems.at[i]) for i, (src, _) in enumerate(pairs)
    ]
    stores = [
        pltpu.make_async_copy(held.at[i], dst, out_sems.at[i]) for i, (_, dst) in enumerate(pairs)
    ]
    for load in loads:
        load.start()
    for load, store in zip(loads, stores):
        load.wait()
        store.start()
    for store in stores:
        store.wait()


def through_scratch(rows, cols, kind):
    return [pltpu.VMEM((FSDP, rows, cols), kind), pltpu.SemaphoreType.DMA((FSDP,)),
            pltpu.SemaphoreType.DMA((FSDP,))]


def regroup_tokens(tokens, step):
    _, _, rows, width = tokens.shape
    cols = width // FSDP

    def body(src, dst, held, in_sems, out_sems):
        through_vmem(
            [(src.at[0, step, :, pl.ds(part * cols, cols)], dst.at[part]) for part in range(FSDP)],
            held, in_sems, out_sems,
        )

    return call(body, "regroup_tokens", None, [], [((FSDP, rows, cols), tokens.dtype)],
                scratch=through_scratch(rows, cols, tokens.dtype), apart=[in_hbm(tokens)],
                out_hbm=True)[0]


def tokens_by_hops(place, tokens, step):
    _, _, rows, width = tokens.shape
    cols = width // FSDP
    groups = (((1, 0), (1, 1)), ((3, 0), (3, 1)), ((0, 1), (2, 1)), ((0, 0),), ((2, 0),))

    def body(place, src, g0, g1, g2, g3, g4, held, in_sems, out_sems):
        pairs = []
        for blocks, dst in zip(groups, (g0, g1, g2, g3, g4)):
            for index, (hops, other) in enumerate(blocks):
                x = 1 - place[1] if other else place[1]
                part = 2 * lax.rem(place[0] + hops, RING) + x
                block = pl.ds(pl.multiple_of(part * cols, cols), cols)
                pairs.append((src.at[0, step, :, block], dst.at[index]))
        through_vmem(pairs, held, in_sems, out_sems)

    return call(body, "tokens_by_hops", place, [],
                [((len(blocks), rows, cols), tokens.dtype) for blocks in groups],
                scratch=through_scratch(rows, cols, tokens.dtype), apart=[in_hbm(tokens)],
                out_hbm=True)


def join_blocks(place, one, one_at, two, two_at):
    _, rows, cols = one.shape

    def body(_, one_hbm, two_hbm, out, sems):
        copies = [
            pltpu.make_async_copy(one_hbm.at[one_at], out.at[0], sems.at[0]),
            pltpu.make_async_copy(two_hbm.at[two_at], out.at[1], sems.at[1]),
        ]
        for copy in copies:
            copy.start()
        for copy in copies:
            copy.wait()

    return call(body, "join_blocks", place, [], [((2, rows, cols), one.dtype)],
                scratch=[pltpu.SemaphoreType.DMA((2,))], apart=[one, two])[0]


def ring_rows(at, hops, count):
    return pl.ds(pl.multiple_of(lax.rem(at + (hops % RING), RING) * count, count), count)


def pair_at(place, tok_refs, hops, cols):
    hops = hops % RING
    if len(tok_refs) > 1:
        places = (((0, 0), (1, 0)), ((2, 0), (5, 0)), ((4, 0), (4, 1)), ((3, 0), (5, 1)))
        return jnp.concatenate(
            [tok_refs[ref][block, :, cols] for ref, block in places[(RING - hops) % RING]], axis=0
        )
    rows = tok_refs[0].shape[0] // FSDP
    first = 2 * lax.rem(place[0] + hops, RING)
    blocks = [
        tok_refs[0][pl.ds(pl.multiple_of((first + x) * rows, rows), rows), cols]
        for x in (place[1], 1 - place[1])
    ]
    return jnp.concatenate(blocks, axis=0)


def keys_outs(mode, rows, cols):
    pair = rows // RING
    if mode == "x":
        return [((rows // 2, cols), f32), ((rows // 2, cols), bf16)]
    kept = {"direct": (), "up": (1,), "down": (3,)}[mode]
    return [((pair, cols), f32)] + [
        ((pair, cols), f32 if hops in kept else bf16) for hops in (1, 2, 3)
    ]


def partial_keys(place, mode, tok_refs, narrow_ref, out_refs):
    every = slice(None)
    for hops in (2, 1, 3, 0):
        part = jnp.dot(
            pair_at(place, tok_refs, hops, every), narrow_ref[...], preferred_element_type=f32
        )
        if mode == "x":
            rows = part.shape[0] // 2
            block = slice(hops * rows, (hops + 1) * rows)
            out_refs[0][block, :] = part[:rows]
            out_refs[1][block, :] = part[rows:].astype(bf16)
        else:
            out_refs[hops][...] = part.astype(out_refs[hops].dtype)


def narrow_chains(place, params, cols):
    width, total = params.shape[1:]
    count = total // cols

    def body(_, w_ref, *out_refs):
        for chain, out_ref in enumerate(out_refs):
            out_ref[...] = w_ref[0, :, chain * cols : (chain + 1) * cols].astype(bf16)

    return call(body, "narrow_chains", place, [params], [((width, cols), bf16)] * count)


def first_keys(place, mode, toks, narrow):
    rows, width = toks.shape
    cols = narrow.shape[1]

    def body(place, tok_ref, narrow_ref, *out_refs):
        partial_keys(place, mode, (tok_ref,), narrow_ref, out_refs)

    return call(body, "first_keys", place, [toks, narrow], keys_outs(mode, rows, cols),
                flops=2 * rows * width * cols)


def add_keys(place, kept, got):
    def body(_, kept_ref, got_ref, out_ref):
        out_ref[...] = (kept_ref[...].astype(f32) + got_ref[...].astype(f32)).astype(bf16)

    return call(body, "add_keys", place, [kept, got], [(kept.shape, bf16)])[0]


def sum_keys(place, own, got, targets, step, chain, inv_root):
    cols = own.shape[1]
    rows = targets.shape[2]

    def body(place, own_ref, *refs):
        got_refs, goal_ref, out_ref = refs[:-2], refs[-2], refs[-1]
        at = slice(chain * cols, (chain + 1) * cols)
        for start in range(0, own.shape[0], rows):
            part = slice(start, start + rows)
            total = own_ref[part, :]
            for ref in got_refs:
                total = total + ref[part, :].astype(f32)
            total = total * inv_root
            if start == 0:
                total = total - goal_ref[0, step, :, at].astype(f32)
            out_ref[part, :] = total.astype(bf16)

    return call(body, "sum_keys", place, [own, *got, targets], [(own.shape, bf16)])[0]


def pair_resid(place, half, other):
    rows = half.shape[0] // 2

    def body(_, half_ref, other_ref, out_ref):
        for mine, theirs in ((slice(0, rows), slice(rows, None)), (slice(rows, None), slice(0, rows))):
            out_ref[mine, :] = (
                half_ref[mine, :].astype(f32) + other_ref[theirs, :].astype(f32)
            ).astype(bf16)

    return call(body, "pair_resid", place, [half, other], [(half.shape, bf16)])[0]


def add_far_keys(place, own, got):
    rows = own.shape[0] // RING
    cols = own.shape[1]

    def body(_, own_ref, got_ref, *out_refs):
        for hops, out_ref in enumerate(out_refs):
            block = slice(hops * rows, (hops + 1) * rows)
            total = own_ref[block, :] + got_ref[block, :].astype(f32)
            out_ref[...] = total.astype(out_ref.dtype)

    return call(body, "add_far_keys", place, [own, got],
                [((rows, cols), f32)] + [((rows, cols), bf16)] * (RING - 1))


def join_pair(place, near, far):
    rows, cols = near.shape

    def body(_, near_ref, far_ref, out_ref):
        out_ref[:rows, :] = near_ref[...]
        out_ref[rows:, :] = far_ref[...]

    return call(body, "join_pair", place, [near, far], [((2 * rows, cols), bf16)])[0]


def resid_at(resid_refs, hops):
    if len(resid_refs) == RING:
        return resid_refs[hops][...]
    return jnp.concatenate([resid_refs[hops][...], resid_refs[RING][hops]], axis=0)


def join_resids(place, resids):
    rows, cols = resids[0].shape

    def body(_, r0, r1, r2, r3, out_ref):
        for hops, ref in enumerate((r0, r1, r2, r3)):
            out_ref[hops] = ref[...]

    return call(body, "join_resids", place, resids, [((RING, rows, cols), bf16)])[0]


def grad_tile(place, tok_refs, resid_refs, tile, inv_root):
    total = None
    for hops in range(RING):
        part = lax.dot_general(
            pair_at(place, tok_refs, -hops, tile),
            resid_at(resid_refs, hops),
            (((0,), (0,)), ((), ())),
            preferred_element_type=f32,
        )
        total = part if total is None else total + part
    return total * inv_root


def adam(grad, first, second, weights):
    first = beta_one * first.astype(f32) + (1.0 - beta_one) * grad
    second = beta_two * second.astype(f32) + (1.0 - beta_two) * grad * grad
    weights = weights - inner_rate * (
        first / (jnp.sqrt(second) + adam_eps) + decay_rate * weights
    )
    return first, second, weights


def middle_step(place, mode, toks, next_toks, resids, params, moment1, moment2, chain, inv_root):
    rows, width = toks.shape
    cols = resids[0].shape[1]
    at = slice(chain * cols, (chain + 1) * cols)

    def body(place, tok_ref, n0, n1, n2, n3, n4, n5, w_ref, m_ref, v_ref, *rest):
        resid_refs, rest = rest[: len(resids)], rest[len(resids) :]
        w_out, m_out, v_out, *out_refs, narrow = rest
        for start in range(0, width, TILE):
            tile = slice(start, start + TILE)
            grad = grad_tile(place, (tok_ref,), resid_refs, tile, inv_root)
            m_new, v_new, w_new = adam(grad, m_ref[0, tile, at], v_ref[0, tile, at], w_ref[0, tile, at])
            w_out[tile, :] = w_new
            m_out[tile, :] = m_new.astype(bf16)
            v_out[tile, :] = v_new.astype(bf16)
            narrow[tile, :] = w_new.astype(bf16)
        partial_keys(place, mode, (n0, n1, n2, n3, n4, n5), narrow, out_refs)

    outs = [((width, cols), f32), ((width, cols), bf16), ((width, cols), bf16)]
    return call(body, "middle_step", place,
                [toks, *next_toks, params, moment1, moment2, *resids],
                outs + keys_outs(mode, rows, cols), scratch=[pltpu.VMEM((width, cols), bf16)],
                flops=4 * rows * width * cols)


def last_step(place, toks, resids, weights, first, second, anchors, chain, inv_root, outs):
    width, cols = weights.shape
    rows = FSDP * toks[0].shape[1]
    slice_rows = width // REP
    at = pl.ds(chain * cols, cols)
    total = 2 * cols

    def body(place, t0, t1, t2, t3, t4, t5, w_ref, m_ref, v_ref, same_ref, other_ref, *rest):
        resid_refs = rest[: len(resids)]
        w_hbm, m_hbm, v_hbm, w_out, m_out, v_out, sems = rest[-7:]
        copies = []
        for index, start in enumerate(range(0, width, TILE)):
            tile = pl.ds(start, TILE)
            grad = grad_tile(place, (t0, t1, t2, t3, t4, t5), resid_refs, tile, inv_root)
            m_new, v_new, w_new = adam(grad, m_ref[tile, :], v_ref[tile, :], w_ref[tile, :])
            m_out[tile, :] = m_new.astype(bf16)
            v_out[tile, :] = v_new.astype(bf16)
            w_out[tile, :] = w_new

            @pl.when(place[5] == chain)
            def _():
                for begin in range(start, start + TILE, slice_rows):
                    owner = begin // slice_rows
                    block = slice(begin, begin + slice_rows)
                    source = slice((owner // 2) * slice_rows, (owner // 2 + 1) * slice_rows)
                    fresh = jnp.where(
                        place[4] == owner % 2,
                        same_ref[source, :].astype(f32),
                        other_ref[source, :].astype(f32),
                    )
                    w_out[block, :] = mix_weight * w_out[block, :] + (1.0 - mix_weight) * fresh

            for which, (src, dst) in enumerate(((w_out, w_hbm), (m_out, m_hbm), (v_out, v_hbm))):
                copy = pltpu.make_async_copy(
                    src.at[tile, :], dst.at[0, tile, at], sems.at[which, index]
                )
                copy.start()
                copies.append(copy)
        for copy in copies:
            copy.wait()

    arrays = [*toks, weights, first, second, *anchors, *resids]
    results = [((1, width, total), f32), ((1, width, total), bf16), ((1, width, total), bf16)]
    aliases = {1 + len(arrays) + i: i for i in range(3)} if outs else {}
    return call(body, "last_step", place, arrays, results, apart=outs, out_hbm=True,
                scratch=[pltpu.VMEM((width, cols), f32), pltpu.VMEM((width, cols), bf16),
                         pltpu.VMEM((width, cols), bf16),
                         pltpu.SemaphoreType.DMA((3, width // TILE))],
                limit=16, flops=2 * rows * width * cols, aliases=aliases)


def delta_for_core(place, delta):
    rows, cols = delta.shape
    part = rows // REP

    def body(place, delta_ref, out_ref):
        for j in range(REP // 2):
            source = pl.ds(pl.multiple_of((2 * j + 1 - place[4]) * part, part), part)
            out_ref[j * part : (j + 1) * part, :] = delta_ref[source, :].astype(bf16)

    return call(body, "delta_for_core", place, [delta], [((rows // 2, cols), bf16)])[0]


def delta_for_ring(place, delta, got):
    rows, cols = delta.shape
    part = rows // REP

    def body(place, delta_ref, got_ref, own_ref, s1, s2, s3):
        for hops in range(RING):
            ring = lax.rem(place[2] + hops, RING)
            for far in range(2):
                j = 2 * ring + far
                near = pl.ds(pl.multiple_of((2 * j + place[4]) * part, part), part)
                sent = pl.ds(pl.multiple_of(j * part, part), part)
                total = delta_ref[near, :] + got_ref[sent, :].astype(f32)
                block = slice(far * part, (far + 1) * part)
                if hops:
                    (s1, s2, s3)[hops - 1][block, :] = total.astype(bf16)
                else:
                    own_ref[block, :] = total

    return call(body, "delta_for_ring", place, [delta, got],
                [((2 * part, cols), f32)] + [((2 * part, cols), bf16)] * (RING - 1))


def delta_for_far(place, own, got, anchor, momentum):
    rows, cols = own.shape
    part = anchor.shape[2]

    def body(place, own_ref, g1, g2, g3, a_ref, p_ref, keep_ref, send_ref):
        total = own_ref[...]
        for ref in (g1, g2, g3):
            total = total + ref[...].astype(f32)
        keep_ref[...] = total
        send_ref[:rows, :] = total.astype(bf16)
        base = a_ref[place[5], 0] - outer_rate * outer_mu * outer_mu * p_ref[place[5], 0]
        send_ref[rows:, :] = base.astype(bf16)

    return call(body, "delta_for_far", place, [own, *got, anchor, momentum],
                [(own.shape, f32), ((rows + part, cols), bf16)])


def outer_step(place, keep, got, anchor, momentum):
    _, _, part, cols = anchor.shape

    def body(place, keep_ref, got_ref, a_ref, p_ref, a_out, p_out, new_ref):
        a_out[...] = a_ref[...]
        p_out[...] = p_ref[...]
        fragment = place[5]
        for far in range(2):
            block = slice(far * part, (far + 1) * part)
            mean = (keep_ref[block, :] + got_ref[block, :].astype(f32)) / REP

            @pl.when(place[3] == far)
            def _():
                moment = outer_mu * p_ref[fragment, 0] + mean
                fresh = a_ref[fragment, 0] - outer_rate * (mean + outer_mu * moment)
                p_out[fragment, 0] = moment
                a_out[fragment, 0] = fresh
                new_ref[block, :] = fresh.astype(bf16)

            @pl.when(place[3] != far)
            def _():
                base = got_ref[2 * part :, :].astype(f32)
                fresh = base - outer_rate * (1.0 + outer_mu) * mean
                new_ref[block, :] = fresh.astype(bf16)

    return call(body, "outer_step", place, [keep, got, anchor, momentum],
                [(anchor.shape, f32), (momentum.shape, f32), (keep.shape, bf16)])


def join_ring(place, pieces):
    part, cols = pieces[0].shape

    def body(place, p0, p1, p2, p3, out_ref):
        for hops, ref in enumerate((p0, p1, p2, p3)):
            out_ref[ring_rows(place[2], RING - hops, part), :] = ref[...]

    return call(body, "join_ring", place, pieces, [((RING * part, cols), bf16)])[0]


class InOrder:
    def __init__(self, place):
        self.place = place

    def __call__(self, kernel, *args):
        results = kernel(self.place, *args)
        single = not isinstance(results, (list, tuple))
        results = [results] if single else list(results)
        results[-1] = self.after(results[-1])
        return results[0] if single else results

    def after(self, value):
        self.place, value = lax.optimization_barrier((self.place, value))
        return value


def by_hops(values):
    return [shift_y(values[hops - 1], hops) for hops in (1, 2, 3)]


def resids_of(run, modes, parts, targets, step, chain, inv_root):
    reduce_mode, gather_mode = modes
    own, *sent = parts
    if reduce_mode == "x":
        own, *sent = run(add_far_keys, own, swap_x(sent[0]))
        got = by_hops(sent)
        yield
        resid = run(sum_keys, own, got, targets, step, chain, inv_root)
        if gather_mode == "x":
            resids = [resid, *by_hops([resid] * 3)]
            yield
            yield [*resids, swap_x(run(join_resids, resids))]
            return
        other = swap_x(resid)
        yield
        resid = run(join_pair, resid, other)
    else:
        k1, k2, k3 = sent
        if reduce_mode == "direct":
            got = by_hops(sent)
        elif reduce_mode == "up":
            relay = run(add_keys, k1, shift_y(k2, 1))
            got = [shift_y(relay, 1), shift_y(k3, 3)]
            yield
        else:
            relay = run(add_keys, k3, shift_y(k2, 3))
            got = [shift_y(relay, 3), shift_y(k1, 1)]
            yield
        half = run(sum_keys, own, got, targets, step, chain, inv_root)
        other = swap_x(half)
        yield
        resid = run(pair_resid, half, other)
    if gather_mode == "direct":
        resids = [resid, *by_hops([resid] * 3)]
    else:
        up, down = shift_y(resid, 1), shift_y(resid, 3)
        resids = [resid, up, shift_y(up, 1) if gather_mode == "up" else shift_y(down, 3), down]
    yield resids


def on_device(tokens, targets, params, moment1, moment2, stale_delta, anchor, momentum, plan):
    inv_root = 1.0 / math.sqrt(tokens.shape[3])
    here = lax.axis_index("fsdp")
    home = lax.axis_index("rep")
    run = InOrder(
        jnp.stack(
            [here // 2, here % 2, home // 4, (home // 2) % 2, home % 2, plan[0]]
        ).astype(jnp.int32)
    )
    cols = stale_delta.shape[2]
    chains = range(params.shape[2] // cols)
    delta = stale_delta[0]

    toks = run.after(regroup_tokens(tokens, 0))
    toks = lax.all_to_all(toks, "fsdp", split_axis=0, concat_axis=0, tiled=True)
    toks = toks.reshape(-1, toks.shape[-1])

    up, down, far, near, opposite = run(tokens_by_hops, tokens, 1)
    up, down, far = shift_y(up, 1), shift_y(down, 3), swap_x(far)
    got = swap_core(run(delta_for_core, delta))
    own, *sent = run(delta_for_ring, delta, got)
    got = [shift_z(sent[h - 1], h) for h in (1, 2, 3)]
    narrow = run(narrow_chains, params, cols)
    keep, send = run(delta_for_far, own, got, anchor, momentum)
    toks = run.after(toks)

    parts = {}
    for chain in chains:
        parts[chain] = run(first_keys, MODES[0][chain][0], toks, narrow[chain])
    steps = [resids_of(run, MODES[0][c], parts[c], targets, 0, c, inv_root) for c in chains]
    resids = {}

    def advance(order):
        nonlocal got, fresh, anchors, next_toks, opposite, sides
        for name in order:
            if name in ("A", "B"):
                chain = ("A", "B").index(name)
                resids[chain] = next(steps[chain])
            elif name == "pairs":
                opposite = shift_y(run(join_blocks, opposite, 0, far, 1), 2)
            elif name == "sides":
                sides = swap_x(run(join_blocks, up, 1, down, 1))
            elif name == "join":
                next_toks = run.after([near, far, up, down, opposite, sides])
            elif name == "outer":
                results.extend(run(outer_step, keep, swap_far(send), anchor, momentum))
                fresh = results.pop()
                up_z, down_z = shift_z(fresh, 1), shift_z(fresh, 3)
                got = [up_z, shift_z(up_z, 1), down_z]
            elif name == "ring":
                fresh = run(join_ring, [fresh, *got])
                anchors = (fresh, swap_core(fresh))

    results = []
    fresh = anchors = next_toks = sides = None
    advance(ORDER[0])
    state = {}
    for chain in chains:
        w, m, v, *parts[chain] = run(
            middle_step, MODES[1][chain][0], toks, next_toks, resids[chain], params, moment1,
            moment2, chain, inv_root
        )
        state[chain] = (w, m, v)
    steps = [resids_of(run, MODES[1][c], parts[c], targets, 1, c, inv_root) for c in chains]
    advance(ORDER[1])
    outs = []
    for chain in chains:
        outs = run(last_step, next_toks, resids[chain], *state[chain], anchors, chain, inv_root, outs)
    return (*outs, *results)


def solution(mesh):
    return jax.shard_map(
        on_device,
        mesh=mesh,
        in_specs=(
            P("rep", None, "fsdp", None),
            P("rep", None, "fsdp", None),
            P("rep", "fsdp", None),
            P("rep", "fsdp", None),
            P("rep", "fsdp", None),
            P("rep", "fsdp", None),
            P(None, "fsdp", "rep", None),
            P(None, "fsdp", "rep", None),
            P(),
        ),
        out_specs=(
            P("rep", "fsdp", None),
            P("rep", "fsdp", None),
            P("rep", "fsdp", None),
            P(None, "fsdp", "rep", None),
            P(None, "fsdp", "rep", None),
        ),
        check_vma=False,
    )
```

```python
import math

import jax
import jax.numpy as jnp
from jax import lax
from jax.experimental import pallas as pl
from jax.experimental.pallas import tpu as pltpu
from jax.sharding import PartitionSpec as P

beta_one = 0.9
beta_two = 0.95
inner_rate = 0.02
decay_rate = 0.1
adam_eps = 1e-08
outer_rate = 0.7
outer_mu = 0.9
mix_weight = 0.5

f32 = jnp.float32
bf16 = jnp.bfloat16

RING = 4
FSDP = 8
REP = 16
TILE = 256
ORDER = (('far', 'sides', 'outer', 'A', 'B', 'A', 'pairs', 'B', 'ring', 'A', 'B', 'join'), ('A', 'B', 'A', 'B'))
MODES = ((('up', 'direct'), ('down', 'direct')), (('direct', 'direct'), ('direct', 'direct')))


def swap_x(value):
    return lax.ppermute(value, "fsdp", [(i, i ^ 1) for i in range(FSDP)])


def shift_y(value, hops):
    return lax.ppermute(value, "fsdp", [(i, (i + 2 * hops) % FSDP) for i in range(FSDP)])


def swap_core(value):
    return lax.ppermute(value, "rep", [(i, i ^ 1) for i in range(REP)])


def swap_far(value):
    return lax.ppermute(value, "rep", [(i, i ^ 2) for i in range(REP)])


def shift_z(value, hops):
    return lax.ppermute(value, "rep", [(i, (i + 4 * hops) % REP) for i in range(REP)])


def in_vmem(value):
    return pltpu.with_memory_space_constraint(value, pltpu.VMEM)


def in_hbm(value):
    return pltpu.with_memory_space_constraint(value, pltpu.HBM)


def call(body, name, place, arrays, outs, scratch=(), limit=8, flops=0, apart=(), out_hbm=False,
         aliases=None):
    vmem = pl.BlockSpec(memory_space=pltpu.VMEM)
    hbm = pl.BlockSpec(memory_space=pl.ANY)
    out = pl.BlockSpec(memory_space=pltpu.HBM) if out_hbm else vmem
    moved = sum(math.prod(a.shape) * a.dtype.itemsize for a in list(arrays) + list(apart))
    moved += sum(math.prod(shape) * jnp.dtype(kind).itemsize for shape, kind in outs)
    return pl.pallas_call(
        body,
        in_specs=[pl.BlockSpec(memory_space=pltpu.SMEM)] * (place is not None)
        + [vmem] * len(arrays) + [hbm] * len(apart),
        out_specs=[out] * len(outs),
        out_shape=[
            (pltpu.HBM if out_hbm else pltpu.VMEM)(shape, kind)
            for shape, kind in outs
        ],
        scratch_shapes=list(scratch),
        input_output_aliases=aliases or {},
        compiler_params=pltpu.CompilerParams(vmem_limit_bytes=limit * 1024 * 1024),
        cost_estimate=pl.CostEstimate(flops=0, bytes_accessed=1024, transcendentals=0),
        name=name,
    )(*([] if place is None else [place]), *[in_vmem(array) for array in arrays], *apart)


def through_vmem(pairs, held, in_sems, out_sems):
    loads = [
        pltpu.make_async_copy(src, held.at[i], in_sems.at[i]) for i, (src, _) in enumerate(pairs)
    ]
    stores = [
        pltpu.make_async_copy(held.at[i], dst, out_sems.at[i]) for i, (_, dst) in enumerate(pairs)
    ]
    for load in loads:
        load.start()
    for load, store in zip(loads, stores):
        load.wait()
        store.start()
    for store in stores:
        store.wait()


def through_scratch(rows, cols, kind):
    return [pltpu.VMEM((FSDP, rows, cols), kind), pltpu.SemaphoreType.DMA((FSDP,)),
            pltpu.SemaphoreType.DMA((FSDP,))]


def regroup_tokens(tokens, step):
    _, _, rows, width = tokens.shape
    cols = width // FSDP

    def body(src, dst, held, in_sems, out_sems):
        through_vmem(
            [(src.at[0, step, :, pl.ds(part * cols, cols)], dst.at[part]) for part in range(FSDP)],
            held, in_sems, out_sems,
        )

    return call(body, "regroup_tokens", None, [], [((FSDP, rows, cols), tokens.dtype)],
                scratch=through_scratch(rows, cols, tokens.dtype), apart=[in_hbm(tokens)],
                out_hbm=True)[0]


def tokens_by_hops(place, tokens, step):
    _, _, rows, width = tokens.shape
    cols = width // FSDP
    groups = (((1, 0), (1, 1)), ((3, 0), (3, 1)), ((0, 1), (2, 1)), ((0, 0),), ((2, 0),))

    def body(place, src, g0, g1, g2, g3, g4, held, in_sems, out_sems):
        pairs = []
        for blocks, dst in zip(groups, (g0, g1, g2, g3, g4)):
            for index, (hops, other) in enumerate(blocks):
                x = 1 - place[1] if other else place[1]
                part = 2 * lax.rem(place[0] + hops, RING) + x
                block = pl.ds(pl.multiple_of(part * cols, cols), cols)
                pairs.append((src.at[0, step, :, block], dst.at[index]))
        through_vmem(pairs, held, in_sems, out_sems)

    return call(body, "tokens_by_hops", place, [],
                [((len(blocks), rows, cols), tokens.dtype) for blocks in groups],
                scratch=through_scratch(rows, cols, tokens.dtype), apart=[in_hbm(tokens)],
                out_hbm=True)


def join_blocks(place, one, one_at, two, two_at):
    _, rows, cols = one.shape

    def body(_, one_hbm, two_hbm, out, sems):
        copies = [
            pltpu.make_async_copy(one_hbm.at[one_at], out.at[0], sems.at[0]),
            pltpu.make_async_copy(two_hbm.at[two_at], out.at[1], sems.at[1]),
        ]
        for copy in copies:
            copy.start()
        for copy in copies:
            copy.wait()

    return call(body, "join_blocks", place, [], [((2, rows, cols), one.dtype)],
                scratch=[pltpu.SemaphoreType.DMA((2,))], apart=[one, two])[0]


def ring_rows(at, hops, count):
    return pl.ds(pl.multiple_of(lax.rem(at + (hops % RING), RING) * count, count), count)


def pair_at(place, tok_refs, hops, cols):
    hops = hops % RING
    if len(tok_refs) > 1:
        places = (((0, 0), (1, 0)), ((2, 0), (5, 0)), ((4, 0), (4, 1)), ((3, 0), (5, 1)))
        return jnp.concatenate(
            [tok_refs[ref][block, :, cols] for ref, block in places[(RING - hops) % RING]], axis=0
        )
    rows = tok_refs[0].shape[0] // FSDP
    first = 2 * lax.rem(place[0] + hops, RING)
    blocks = [
        tok_refs[0][pl.ds(pl.multiple_of((first + x) * rows, rows), rows), cols]
        for x in (place[1], 1 - place[1])
    ]
    return jnp.concatenate(blocks, axis=0)


def keys_outs(mode, rows, cols):
    pair = rows // RING
    if mode == "x":
        return [((rows // 2, cols), f32), ((rows // 2, cols), bf16)]
    kept = {"direct": (), "up": (1,), "down": (3,)}[mode]
    return [((pair, cols), f32)] + [
        ((pair, cols), f32 if hops in kept else bf16) for hops in (1, 2, 3)
    ]


def partial_keys(place, mode, tok_refs, narrow_ref, out_refs):
    every = slice(None)
    for hops in (2, 1, 3, 0):
        part = jnp.dot(
            pair_at(place, tok_refs, hops, every), narrow_ref[...], preferred_element_type=f32
        )
        if mode == "x":
            rows = part.shape[0] // 2
            block = slice(hops * rows, (hops + 1) * rows)
            out_refs[0][block, :] = part[:rows]
            out_refs[1][block, :] = part[rows:].astype(bf16)
        else:
            out_refs[hops][...] = part.astype(out_refs[hops].dtype)


def narrow_chains(place, params, cols):
    width, total = params.shape[1:]
    count = total // cols

    def body(_, w_ref, *out_refs):
        for chain, out_ref in enumerate(out_refs):
            out_ref[...] = w_ref[0, :, chain * cols : (chain + 1) * cols].astype(bf16)

    return call(body, "narrow_chains", place, [params], [((width, cols), bf16)] * count)


def first_keys(place, mode, toks, narrow):
    rows, width = toks.shape
    cols = narrow.shape[1]

    def body(place, tok_ref, narrow_ref, *out_refs):
        partial_keys(place, mode, (tok_ref,), narrow_ref, out_refs)

    return call(body, "first_keys", place, [toks, narrow], keys_outs(mode, rows, cols),
                flops=2 * rows * width * cols)


def add_keys(place, kept, got):
    def body(_, kept_ref, got_ref, out_ref):
        out_ref[...] = (kept_ref[...].astype(f32) + got_ref[...].astype(f32)).astype(bf16)

    return call(body, "add_keys", place, [kept, got], [(kept.shape, bf16)])[0]


def sum_keys(place, own, got, targets, step, chain, inv_root):
    cols = own.shape[1]
    rows = targets.shape[2]

    def body(place, own_ref, *refs):
        got_refs, goal_ref, out_ref = refs[:-2], refs[-2], refs[-1]
        at = slice(chain * cols, (chain + 1) * cols)
        for start in range(0, own.shape[0], rows):
            part = slice(start, start + rows)
            total = own_ref[part, :]
            for ref in got_refs:
                total = total + ref[part, :].astype(f32)
            total = total * inv_root
            if start == 0:
                total = total - goal_ref[0, step, :, at].astype(f32)
            out_ref[part, :] = total.astype(bf16)

    return call(body, "sum_keys", place, [own, *got, targets], [(own.shape, bf16)])[0]


def pair_resid(place, half, other):
    rows = half.shape[0] // 2

    def body(_, half_ref, other_ref, out_ref):
        for mine, theirs in ((slice(0, rows), slice(rows, None)), (slice(rows, None), slice(0, rows))):
            out_ref[mine, :] = (
                half_ref[mine, :].astype(f32) + other_ref[theirs, :].astype(f32)
            ).astype(bf16)

    return call(body, "pair_resid", place, [half, other], [(half.shape, bf16)])[0]


def add_far_keys(place, own, got):
    rows = own.shape[0] // RING
    cols = own.shape[1]

    def body(_, own_ref, got_ref, *out_refs):
        for hops, out_ref in enumerate(out_refs):
            block = slice(hops * rows, (hops + 1) * rows)
            total = own_ref[block, :] + got_ref[block, :].astype(f32)
            out_ref[...] = total.astype(out_ref.dtype)

    return call(body, "add_far_keys", place, [own, got],
                [((rows, cols), f32)] + [((rows, cols), bf16)] * (RING - 1))


def join_pair(place, near, far):
    rows, cols = near.shape

    def body(_, near_ref, far_ref, out_ref):
        out_ref[:rows, :] = near_ref[...]
        out_ref[rows:, :] = far_ref[...]

    return call(body, "join_pair", place, [near, far], [((2 * rows, cols), bf16)])[0]


def resid_at(resid_refs, hops):
    if len(resid_refs) == RING:
        return resid_refs[hops][...]
    return jnp.concatenate([resid_refs[hops][...], resid_refs[RING][hops]], axis=0)


def join_resids(place, resids):
    rows, cols = resids[0].shape

    def body(_, r0, r1, r2, r3, out_ref):
        for hops, ref in enumerate((r0, r1, r2, r3)):
            out_ref[hops] = ref[...]

    return call(body, "join_resids", place, resids, [((RING, rows, cols), bf16)])[0]


def grad_tile(place, tok_refs, resid_refs, tile, inv_root):
    total = None
    for hops in range(RING):
        part = lax.dot_general(
            pair_at(place, tok_refs, -hops, tile),
            resid_at(resid_refs, hops),
            (((0,), (0,)), ((), ())),
            preferred_element_type=f32,
        )
        total = part if total is None else total + part
    return total * inv_root


def adam(grad, first, second, weights):
    first = beta_one * first.astype(f32) + (1.0 - beta_one) * grad
    second = beta_two * second.astype(f32) + (1.0 - beta_two) * grad * grad
    weights = weights - inner_rate * (
        first / (jnp.sqrt(second) + adam_eps) + decay_rate * weights
    )
    return first, second, weights


def middle_step(place, mode, toks, next_toks, resids, params, moment1, moment2, chain, inv_root):
    rows, width = toks.shape
    cols = resids[0].shape[1]
    at = slice(chain * cols, (chain + 1) * cols)

    def body(place, tok_ref, n0, n1, n2, n3, n4, n5, w_ref, m_ref, v_ref, *rest):
        resid_refs, rest = rest[: len(resids)], rest[len(resids) :]
        w_out, m_out, v_out, *out_refs, narrow = rest
        for start in range(0, width, TILE):
            tile = slice(start, start + TILE)
            grad = grad_tile(place, (tok_ref,), resid_refs, tile, inv_root)
            m_new, v_new, w_new = adam(grad, m_ref[0, tile, at], v_ref[0, tile, at], w_ref[0, tile, at])
            w_out[tile, :] = w_new
            m_out[tile, :] = m_new.astype(bf16)
            v_out[tile, :] = v_new.astype(bf16)
            narrow[tile, :] = w_new.astype(bf16)
        partial_keys(place, mode, (n0, n1, n2, n3, n4, n5), narrow, out_refs)

    outs = [((width, cols), f32), ((width, cols), bf16), ((width, cols), bf16)]
    return call(body, "middle_step", place,
                [toks, *next_toks, params, moment1, moment2, *resids],
                outs + keys_outs(mode, rows, cols), scratch=[pltpu.VMEM((width, cols), bf16)],
                flops=4 * rows * width * cols)


def last_step(place, toks, resids, weights, first, second, anchors, chain, inv_root, outs):
    width, cols = weights.shape
    rows = FSDP * toks[0].shape[1]
    slice_rows = width // REP
    at = pl.ds(chain * cols, cols)
    total = 2 * cols

    def body(place, t0, t1, t2, t3, t4, t5, w_ref, m_ref, v_ref, same_ref, other_ref, *rest):
        resid_refs = rest[: len(resids)]
        w_hbm, m_hbm, v_hbm, w_out, m_out, v_out, sems = rest[-7:]
        copies = []
        for index, start in enumerate(range(0, width, TILE)):
            tile = pl.ds(start, TILE)
            grad = grad_tile(place, (t0, t1, t2, t3, t4, t5), resid_refs, tile, inv_root)
            m_new, v_new, w_new = adam(grad, m_ref[tile, :], v_ref[tile, :], w_ref[tile, :])
            m_out[tile, :] = m_new.astype(bf16)
            v_out[tile, :] = v_new.astype(bf16)
            w_out[tile, :] = w_new

            @pl.when(place[5] == chain)
            def _():
                for begin in range(start, start + TILE, slice_rows):
                    owner = begin // slice_rows
                    block = slice(begin, begin + slice_rows)
                    source = slice((owner // 2) * slice_rows, (owner // 2 + 1) * slice_rows)
                    fresh = jnp.where(
                        place[4] == owner % 2,
                        same_ref[source, :].astype(f32),
                        other_ref[source, :].astype(f32),
                    )
                    w_out[block, :] = mix_weight * w_out[block, :] + (1.0 - mix_weight) * fresh

            for which, (src, dst) in enumerate(((w_out, w_hbm), (m_out, m_hbm), (v_out, v_hbm))):
                copy = pltpu.make_async_copy(
                    src.at[tile, :], dst.at[0, tile, at], sems.at[which, index]
                )
                copy.start()
                copies.append(copy)
        for copy in copies:
            copy.wait()

    arrays = [*toks, weights, first, second, *anchors, *resids]
    results = [((1, width, total), f32), ((1, width, total), bf16), ((1, width, total), bf16)]
    aliases = {1 + len(arrays) + i: i for i in range(3)} if outs else {}
    return call(body, "last_step", place, arrays, results, apart=outs, out_hbm=True,
                scratch=[pltpu.VMEM((width, cols), f32), pltpu.VMEM((width, cols), bf16),
                         pltpu.VMEM((width, cols), bf16),
                         pltpu.SemaphoreType.DMA((3, width // TILE))],
                limit=16, flops=2 * rows * width * cols, aliases=aliases)


def delta_for_core(place, delta):
    rows, cols = delta.shape
    part = rows // REP

    def body(place, delta_ref, out_ref):
        for j in range(REP // 2):
            source = pl.ds(pl.multiple_of((2 * j + 1 - place[4]) * part, part), part)
            out_ref[j * part : (j + 1) * part, :] = delta_ref[source, :].astype(bf16)

    return call(body, "delta_for_core", place, [delta], [((rows // 2, cols), bf16)])[0]


def delta_for_ring(place, delta, got):
    rows, cols = delta.shape
    part = rows // REP

    def body(place, delta_ref, got_ref, own_ref, s1, s2, s3):
        for hops in range(RING):
            ring = lax.rem(place[2] + hops, RING)
            for far in range(2):
                j = 2 * ring + far
                near = pl.ds(pl.multiple_of((2 * j + place[4]) * part, part), part)
                sent = pl.ds(pl.multiple_of(j * part, part), part)
                total = delta_ref[near, :] + got_ref[sent, :].astype(f32)
                block = slice(far * part, (far + 1) * part)
                if hops:
                    (s1, s2, s3)[hops - 1][block, :] = total.astype(bf16)
                else:
                    own_ref[block, :] = total

    return call(body, "delta_for_ring", place, [delta, got],
                [((2 * part, cols), f32)] + [((2 * part, cols), bf16)] * (RING - 1))


def delta_for_far(place, own, got, anchor, momentum):
    rows, cols = own.shape
    part = anchor.shape[2]

    def body(place, own_ref, g1, g2, g3, a_ref, p_ref, keep_ref, send_ref):
        total = own_ref[...]
        for ref in (g1, g2, g3):
            total = total + ref[...].astype(f32)
        keep_ref[...] = total
        send_ref[:rows, :] = total.astype(bf16)
        base = a_ref[place[5], 0] - outer_rate * outer_mu * outer_mu * p_ref[place[5], 0]
        send_ref[rows:, :] = base.astype(bf16)

    return call(body, "delta_for_far", place, [own, *got, anchor, momentum],
                [(own.shape, f32), ((rows + part, cols), bf16)])


def outer_step(place, keep, got, anchor, momentum):
    _, _, part, cols = anchor.shape

    def body(place, keep_ref, got_ref, a_ref, p_ref, a_out, p_out, new_ref):
        a_out[...] = a_ref[...]
        p_out[...] = p_ref[...]
        fragment = place[5]
        for far in range(2):
            block = slice(far * part, (far + 1) * part)
            mean = (keep_ref[block, :] + got_ref[block, :].astype(f32)) / REP

            @pl.when(place[3] == far)
            def _():
                moment = outer_mu * p_ref[fragment, 0] + mean
                fresh = a_ref[fragment, 0] - outer_rate * (mean + outer_mu * moment)
                p_out[fragment, 0] = moment
                a_out[fragment, 0] = fresh
                new_ref[block, :] = fresh.astype(bf16)

            @pl.when(place[3] != far)
            def _():
                base = got_ref[2 * part :, :].astype(f32)
                fresh = base - outer_rate * (1.0 + outer_mu) * mean
                new_ref[block, :] = fresh.astype(bf16)

    return call(body, "outer_step", place, [keep, got, anchor, momentum],
                [(anchor.shape, f32), (momentum.shape, f32), (keep.shape, bf16)])


def join_ring(place, pieces):
    part, cols = pieces[0].shape

    def body(place, p0, p1, p2, p3, out_ref):
        for hops, ref in enumerate((p0, p1, p2, p3)):
            out_ref[ring_rows(place[2], RING - hops, part), :] = ref[...]

    return call(body, "join_ring", place, pieces, [((RING * part, cols), bf16)])[0]


class InOrder:
    def __init__(self, place):
        self.place = place

    def __call__(self, kernel, *args):
        results = kernel(self.place, *args)
        single = not isinstance(results, (list, tuple))
        results = [results] if single else list(results)
        results[-1] = self.after(results[-1])
        return results[0] if single else results

    def after(self, value):
        self.place, value = lax.optimization_barrier((self.place, value))
        return value


def by_hops(values):
    return [shift_y(values[hops - 1], hops) for hops in (1, 2, 3)]


def resids_of(run, modes, parts, targets, step, chain, inv_root):
    reduce_mode, gather_mode = modes
    own, *sent = parts
    if reduce_mode == "x":
        own, *sent = run(add_far_keys, own, swap_x(sent[0]))
        got = by_hops(sent)
        yield
        resid = run(sum_keys, own, got, targets, step, chain, inv_root)
        if gather_mode == "x":
            resids = [resid, *by_hops([resid] * 3)]
            yield
            yield [*resids, swap_x(run(join_resids, resids))]
            return
        other = swap_x(resid)
        yield
        resid = run(join_pair, resid, other)
    else:
        k1, k2, k3 = sent
        if reduce_mode == "direct":
            got = by_hops(sent)
        elif reduce_mode == "up":
            relay = run(add_keys, k1, shift_y(k2, 1))
            got = [shift_y(relay, 1), shift_y(k3, 3)]
            yield
        else:
            relay = run(add_keys, k3, shift_y(k2, 3))
            got = [shift_y(relay, 3), shift_y(k1, 1)]
            yield
        half = run(sum_keys, own, got, targets, step, chain, inv_root)
        other = swap_x(half)
        yield
        resid = run(pair_resid, half, other)
    if gather_mode == "direct":
        resids = [resid, *by_hops([resid] * 3)]
    else:
        up, down = shift_y(resid, 1), shift_y(resid, 3)
        resids = [resid, up, shift_y(up, 1) if gather_mode == "up" else shift_y(down, 3), down]
    yield resids


def on_device(tokens, targets, params, moment1, moment2, stale_delta, anchor, momentum, plan):
    inv_root = 1.0 / math.sqrt(tokens.shape[3])
    here = lax.axis_index("fsdp")
    home = lax.axis_index("rep")
    run = InOrder(
        jnp.stack(
            [here // 2, here % 2, home // 4, (home // 2) % 2, home % 2, plan[0]]
        ).astype(jnp.int32)
    )
    cols = stale_delta.shape[2]
    chains = range(params.shape[2] // cols)
    delta = stale_delta[0]

    toks = run.after(regroup_tokens(tokens, 0))
    toks = lax.all_to_all(toks, "fsdp", split_axis=0, concat_axis=0, tiled=True)
    toks = toks.reshape(-1, toks.shape[-1])

    up, down, far, near, opposite = run(tokens_by_hops, tokens, 1)
    up, down, far = shift_y(up, 1), shift_y(down, 3), swap_x(far)
    got = swap_core(run(delta_for_core, delta))
    own, *sent = run(delta_for_ring, delta, got)
    got = [shift_z(sent[h - 1], h) for h in (1, 2, 3)]
    narrow = run(narrow_chains, params, cols)
    keep, send = run(delta_for_far, own, got, anchor, momentum)
    toks = run.after(toks)

    parts = {}
    for chain in chains:
        parts[chain] = run(first_keys, MODES[0][chain][0], toks, narrow[chain])
    steps = [resids_of(run, MODES[0][c], parts[c], targets, 0, c, inv_root) for c in chains]
    resids = {}

    def advance(order):
        nonlocal got, fresh, anchors, next_toks, opposite, sides, far
        for name in order:
            if name in ("A", "B"):
                chain = ("A", "B").index(name)
                resids[chain] = next(steps[chain])
            elif name == "pairs":
                opposite = shift_y(run(join_blocks, opposite, 0, far, 1), 2)
            elif name == "far":
                far = run.after(far)
            elif name == "sides":
                sides = swap_x(run(join_blocks, up, 1, down, 1))
            elif name == "join":
                next_toks = run.after([near, far, up, down, opposite, sides])
            elif name == "outer":
                results.extend(run(outer_step, keep, swap_far(send), anchor, momentum))
                fresh = results.pop()
                up_z, down_z = shift_z(fresh, 1), shift_z(fresh, 3)
                got = [up_z, shift_z(up_z, 1), down_z]
            elif name == "ring":
                fresh = run(join_ring, [fresh, *got])
                anchors = (fresh, swap_core(fresh))

    results = []
    fresh = anchors = next_toks = sides = None
    advance(ORDER[0])
    state = {}
    for chain in chains:
        w, m, v, *parts[chain] = run(
            middle_step, MODES[1][chain][0], toks, next_toks, resids[chain], params, moment1,
            moment2, chain, inv_root
        )
        state[chain] = (w, m, v)
    steps = [resids_of(run, MODES[1][c], parts[c], targets, 1, c, inv_root) for c in chains]
    advance(ORDER[1])
    outs = []
    for chain in chains:
        outs = run(last_step, next_toks, resids[chain], *state[chain], anchors, chain, inv_root, outs)
    return (*outs, *results)


def solution(mesh):
    return jax.shard_map(
        on_device,
        mesh=mesh,
        in_specs=(
            P("rep", None, "fsdp", None),
            P("rep", None, "fsdp", None),
            P("rep", "fsdp", None),
            P("rep", "fsdp", None),
            P("rep", "fsdp", None),
            P("rep", "fsdp", None),
            P(None, "fsdp", "rep", None),
            P(None, "fsdp", "rep", None),
            P(),
        ),
        out_specs=(
            P("rep", "fsdp", None),
            P("rep", "fsdp", None),
            P("rep", "fsdp", None),
            P(None, "fsdp", "rep", None),
            P(None, "fsdp", "rep", None),
        ),
        check_vma=False,
    )
```

```python
import math

import jax
import jax.numpy as jnp
from jax import lax
from jax.experimental import pallas as pl
from jax.experimental.pallas import tpu as pltpu
from jax.sharding import PartitionSpec as P

beta_one = 0.9
beta_two = 0.95
inner_rate = 0.02
decay_rate = 0.1
adam_eps = 1e-08
outer_rate = 0.7
outer_mu = 0.9
mix_weight = 0.5

f32 = jnp.float32
bf16 = jnp.bfloat16

RING = 4
FSDP = 8
REP = 16
TILE = 256
ORDER = (('far', 'sides', 'outer', 'A', 'B', 'A', 'pairs', 'B', 'ring', 'A', 'B', 'join'), ('A', 'B', 'A', 'B'))
MODES = ((('up', 'direct'), ('down', 'direct')), (('direct', 'direct'), ('direct', 'direct')))


def swap_x(value):
    return lax.ppermute(value, "fsdp", [(i, i ^ 1) for i in range(FSDP)])


def shift_y(value, hops):
    return lax.ppermute(value, "fsdp", [(i, (i + 2 * hops) % FSDP) for i in range(FSDP)])


def swap_core(value):
    return lax.ppermute(value, "rep", [(i, i ^ 1) for i in range(REP)])


def swap_far(value):
    return lax.ppermute(value, "rep", [(i, i ^ 2) for i in range(REP)])


def shift_z(value, hops):
    return lax.ppermute(value, "rep", [(i, (i + 4 * hops) % REP) for i in range(REP)])


def in_vmem(value):
    return pltpu.with_memory_space_constraint(value, pltpu.VMEM)


def in_hbm(value):
    return pltpu.with_memory_space_constraint(value, pltpu.HBM)


def call(body, name, place, arrays, outs, scratch=(), limit=8, flops=0, apart=(), out_hbm=False,
         aliases=None):
    vmem = pl.BlockSpec(memory_space=pltpu.VMEM)
    hbm = pl.BlockSpec(memory_space=pl.ANY)
    out = pl.BlockSpec(memory_space=pltpu.HBM) if out_hbm else vmem
    moved = sum(math.prod(a.shape) * a.dtype.itemsize for a in list(arrays) + list(apart))
    moved += sum(math.prod(shape) * jnp.dtype(kind).itemsize for shape, kind in outs)
    return pl.pallas_call(
        body,
        in_specs=[pl.BlockSpec(memory_space=pltpu.SMEM)] * (place is not None)
        + [vmem] * len(arrays) + [hbm] * len(apart),
        out_specs=[out] * len(outs),
        out_shape=[
            (pltpu.HBM if out_hbm else pltpu.VMEM)(shape, kind)
            for shape, kind in outs
        ],
        scratch_shapes=list(scratch),
        input_output_aliases=aliases or {},
        compiler_params=pltpu.CompilerParams(vmem_limit_bytes=limit * 1024 * 1024),
        cost_estimate=pl.CostEstimate(flops=0, bytes_accessed=1024, transcendentals=0),
        name=name,
    )(*([] if place is None else [place]), *[in_vmem(array) for array in arrays], *apart)


def through_vmem(pairs, held, in_sems, out_sems):
    loads = [
        pltpu.make_async_copy(src, held.at[i], in_sems.at[i]) for i, (src, _) in enumerate(pairs)
    ]
    stores = [
        pltpu.make_async_copy(held.at[i], dst, out_sems.at[i]) for i, (_, dst) in enumerate(pairs)
    ]
    for load in loads:
        load.start()
    for load, store in zip(loads, stores):
        load.wait()
        store.start()
    for store in stores:
        store.wait()


def through_scratch(rows, cols, kind):
    return [pltpu.VMEM((FSDP, rows, cols), kind), pltpu.SemaphoreType.DMA((FSDP,)),
            pltpu.SemaphoreType.DMA((FSDP,))]


def regroup_tokens(tokens, step):
    _, _, rows, width = tokens.shape
    cols = width // FSDP

    def body(src, dst, held, in_sems, out_sems):
        through_vmem(
            [(src.at[0, step, :, pl.ds(part * cols, cols)], dst.at[part]) for part in range(FSDP)],
            held, in_sems, out_sems,
        )

    return call(body, "regroup_tokens", None, [], [((FSDP, rows, cols), tokens.dtype)],
                scratch=through_scratch(rows, cols, tokens.dtype), apart=[in_hbm(tokens)],
                out_hbm=True)[0]


def tokens_by_hops(place, tokens, step):
    _, _, rows, width = tokens.shape
    cols = width // FSDP
    groups = (((1, 0), (1, 1)), ((3, 0), (3, 1)), ((0, 1), (2, 1)), ((0, 0),), ((2, 0),))

    def body(place, src, g0, g1, g2, g3, g4, held, in_sems, out_sems):
        pairs = []
        for blocks, dst in zip(groups, (g0, g1, g2, g3, g4)):
            for index, (hops, other) in enumerate(blocks):
                x = 1 - place[1] if other else place[1]
                part = 2 * lax.rem(place[0] + hops, RING) + x
                block = pl.ds(pl.multiple_of(part * cols, cols), cols)
                pairs.append((src.at[0, step, :, block], dst.at[index]))
        through_vmem(pairs, held, in_sems, out_sems)

    return call(body, "tokens_by_hops", place, [],
                [((len(blocks), rows, cols), tokens.dtype) for blocks in groups],
                scratch=through_scratch(rows, cols, tokens.dtype), apart=[in_hbm(tokens)],
                out_hbm=True)


def join_blocks(place, one, one_at, two, two_at):
    _, rows, cols = one.shape

    def body(_, one_hbm, two_hbm, out, sems):
        copies = [
            pltpu.make_async_copy(one_hbm.at[one_at], out.at[0], sems.at[0]),
            pltpu.make_async_copy(two_hbm.at[two_at], out.at[1], sems.at[1]),
        ]
        for copy in copies:
            copy.start()
        for copy in copies:
            copy.wait()

    return call(body, "join_blocks", place, [], [((2, rows, cols), one.dtype)],
                scratch=[pltpu.SemaphoreType.DMA((2,))], apart=[one, two])[0]


def ring_rows(at, hops, count):
    return pl.ds(pl.multiple_of(lax.rem(at + (hops % RING), RING) * count, count), count)


def pair_at(place, tok_refs, hops, cols):
    hops = hops % RING
    if len(tok_refs) > 1:
        places = (((0, 0), (1, 0)), ((2, 0), (5, 0)), ((4, 0), (4, 1)), ((3, 0), (5, 1)))
        return jnp.concatenate(
            [tok_refs[ref][block, :, cols] for ref, block in places[(RING - hops) % RING]], axis=0
        )
    rows = tok_refs[0].shape[0] // FSDP
    first = 2 * lax.rem(place[0] + hops, RING)
    blocks = [
        tok_refs[0][pl.ds(pl.multiple_of((first + x) * rows, rows), rows), cols]
        for x in (place[1], 1 - place[1])
    ]
    return jnp.concatenate(blocks, axis=0)


def keys_outs(mode, rows, cols):
    pair = rows // RING
    if mode == "x":
        return [((rows // 2, cols), f32), ((rows // 2, cols), bf16)]
    kept = {"direct": (), "up": (1,), "down": (3,)}[mode]
    return [((pair, cols), f32)] + [
        ((pair, cols), f32 if hops in kept else bf16) for hops in (1, 2, 3)
    ]


def partial_keys(place, mode, tok_refs, narrow_ref, out_refs):
    every = slice(None)
    for hops in (2, 1, 3, 0):
        part = jnp.dot(
            pair_at(place, tok_refs, hops, every), narrow_ref[...], preferred_element_type=f32
        )
        if mode == "x":
            rows = part.shape[0] // 2
            block = slice(hops * rows, (hops + 1) * rows)
            out_refs[0][block, :] = part[:rows]
            out_refs[1][block, :] = part[rows:].astype(bf16)
        else:
            out_refs[hops][...] = part.astype(out_refs[hops].dtype)


def narrow_chains(place, params, cols):
    width, total = params.shape[1:]
    count = total // cols

    def body(_, w_ref, *out_refs):
        for chain, out_ref in enumerate(out_refs):
            out_ref[...] = w_ref[0, :, chain * cols : (chain + 1) * cols].astype(bf16)

    return call(body, "narrow_chains", place, [params], [((width, cols), bf16)] * count)


def first_keys(place, mode, toks, narrow):
    rows, width = toks.shape
    cols = narrow.shape[1]

    def body(place, tok_ref, narrow_hbm, *rest):
        *out_refs, held, sem = rest
        copy = pltpu.make_async_copy(narrow_hbm, held, sem)
        copy.start()
        copy.wait()
        partial_keys(place, mode, (tok_ref,), held, out_refs)

    return call(body, "first_keys", place, [toks], keys_outs(mode, rows, cols), apart=[narrow],
                scratch=[pltpu.VMEM((width, cols), bf16), pltpu.SemaphoreType.DMA(())],
                flops=2 * rows * width * cols)


def add_keys(place, kept, got):
    def body(_, kept_ref, got_ref, out_ref):
        out_ref[...] = (kept_ref[...].astype(f32) + got_ref[...].astype(f32)).astype(bf16)

    return call(body, "add_keys", place, [kept, got], [(kept.shape, bf16)])[0]


def sum_keys(place, own, got, targets, step, chain, inv_root):
    cols = own.shape[1]
    rows = targets.shape[2]

    def body(place, own_ref, *refs):
        got_refs, goal_ref, out_ref = refs[:-2], refs[-2], refs[-1]
        at = slice(chain * cols, (chain + 1) * cols)
        for start in range(0, own.shape[0], rows):
            part = slice(start, start + rows)
            total = own_ref[part, :]
            for ref in got_refs:
                total = total + ref[part, :].astype(f32)
            total = total * inv_root
            if start == 0:
                total = total - goal_ref[0, step, :, at].astype(f32)
            out_ref[part, :] = total.astype(bf16)

    return call(body, "sum_keys", place, [own, *got, targets], [(own.shape, bf16)])[0]


def pair_resid(place, half, other):
    rows = half.shape[0] // 2

    def body(_, half_ref, other_ref, out_ref):
        for mine, theirs in ((slice(0, rows), slice(rows, None)), (slice(rows, None), slice(0, rows))):
            out_ref[mine, :] = (
                half_ref[mine, :].astype(f32) + other_ref[theirs, :].astype(f32)
            ).astype(bf16)

    return call(body, "pair_resid", place, [half, other], [(half.shape, bf16)])[0]


def add_far_keys(place, own, got):
    rows = own.shape[0] // RING
    cols = own.shape[1]

    def body(_, own_ref, got_ref, *out_refs):
        for hops, out_ref in enumerate(out_refs):
            block = slice(hops * rows, (hops + 1) * rows)
            total = own_ref[block, :] + got_ref[block, :].astype(f32)
            out_ref[...] = total.astype(out_ref.dtype)

    return call(body, "add_far_keys", place, [own, got],
                [((rows, cols), f32)] + [((rows, cols), bf16)] * (RING - 1))


def join_pair(place, near, far):
    rows, cols = near.shape

    def body(_, near_ref, far_ref, out_ref):
        out_ref[:rows, :] = near_ref[...]
        out_ref[rows:, :] = far_ref[...]

    return call(body, "join_pair", place, [near, far], [((2 * rows, cols), bf16)])[0]


def resid_at(resid_refs, hops):
    if len(resid_refs) == RING:
        return resid_refs[hops][...]
    return jnp.concatenate([resid_refs[hops][...], resid_refs[RING][hops]], axis=0)


def join_resids(place, resids):
    rows, cols = resids[0].shape

    def body(_, r0, r1, r2, r3, out_ref):
        for hops, ref in enumerate((r0, r1, r2, r3)):
            out_ref[hops] = ref[...]

    return call(body, "join_resids", place, resids, [((RING, rows, cols), bf16)])[0]


def grad_tile(place, tok_refs, resid_refs, tile, inv_root):
    total = None
    for hops in range(RING):
        part = lax.dot_general(
            pair_at(place, tok_refs, -hops, tile),
            resid_at(resid_refs, hops),
            (((0,), (0,)), ((), ())),
            preferred_element_type=f32,
        )
        total = part if total is None else total + part
    return total * inv_root


def adam(grad, first, second, weights):
    first = beta_one * first.astype(f32) + (1.0 - beta_one) * grad
    second = beta_two * second.astype(f32) + (1.0 - beta_two) * grad * grad
    weights = weights - inner_rate * (
        first / (jnp.sqrt(second) + adam_eps) + decay_rate * weights
    )
    return first, second, weights


def middle_step(place, mode, toks, next_toks, resids, params, moment1, moment2, chain, inv_root):
    rows, width = toks.shape
    cols = resids[0].shape[1]
    at = slice(chain * cols, (chain + 1) * cols)

    def body(place, tok_ref, n0, n1, n2, n3, n4, n5, w_ref, m_ref, v_ref, *rest):
        resid_refs, rest = rest[: len(resids)], rest[len(resids) :]
        w_out, m_out, v_out, *out_refs, narrow = rest
        for start in range(0, width, TILE):
            tile = slice(start, start + TILE)
            grad = grad_tile(place, (tok_ref,), resid_refs, tile, inv_root)
            m_new, v_new, w_new = adam(grad, m_ref[0, tile, at], v_ref[0, tile, at], w_ref[0, tile, at])
            w_out[tile, :] = w_new
            m_out[tile, :] = m_new.astype(bf16)
            v_out[tile, :] = v_new.astype(bf16)
            narrow[tile, :] = w_new.astype(bf16)
        partial_keys(place, mode, (n0, n1, n2, n3, n4, n5), narrow, out_refs)

    outs = [((width, cols), f32), ((width, cols), bf16), ((width, cols), bf16)]
    return call(body, "middle_step", place,
                [toks, *next_toks, params, moment1, moment2, *resids],
                outs + keys_outs(mode, rows, cols), scratch=[pltpu.VMEM((width, cols), bf16)],
                flops=4 * rows * width * cols)


def last_step(place, toks, resids, weights, first, second, anchors, chain, inv_root, outs):
    width, cols = weights.shape
    rows = FSDP * toks[0].shape[1]
    slice_rows = width // REP
    at = pl.ds(chain * cols, cols)
    total = 2 * cols

    def body(place, t0, t1, t2, t3, t4, t5, w_ref, m_ref, v_ref, same_ref, other_ref, *rest):
        resid_refs = rest[: len(resids)]
        w_hbm, m_hbm, v_hbm, w_out, m_out, v_out, sems = rest[-7:]
        copies = []
        for index, start in enumerate(range(0, width, TILE)):
            tile = pl.ds(start, TILE)
            grad = grad_tile(place, (t0, t1, t2, t3, t4, t5), resid_refs, tile, inv_root)
            m_new, v_new, w_new = adam(grad, m_ref[tile, :], v_ref[tile, :], w_ref[tile, :])
            m_out[tile, :] = m_new.astype(bf16)
            v_out[tile, :] = v_new.astype(bf16)
            w_out[tile, :] = w_new

            @pl.when(place[5] == chain)
            def _():
                for begin in range(start, start + TILE, slice_rows):
                    owner = begin // slice_rows
                    block = slice(begin, begin + slice_rows)
                    source = slice((owner // 2) * slice_rows, (owner // 2 + 1) * slice_rows)
                    fresh = jnp.where(
                        place[4] == owner % 2,
                        same_ref[source, :].astype(f32),
                        other_ref[source, :].astype(f32),
                    )
                    w_out[block, :] = mix_weight * w_out[block, :] + (1.0 - mix_weight) * fresh

            for which, (src, dst) in enumerate(((w_out, w_hbm), (m_out, m_hbm), (v_out, v_hbm))):
                copy = pltpu.make_async_copy(
                    src.at[tile, :], dst.at[0, tile, at], sems.at[which, index]
                )
                copy.start()
                copies.append(copy)
        for copy in copies:
            copy.wait()

    arrays = [*toks, weights, first, second, *anchors, *resids]
    results = [((1, width, total), f32), ((1, width, total), bf16), ((1, width, total), bf16)]
    aliases = {1 + len(arrays) + i: i for i in range(3)} if outs else {}
    return call(body, "last_step", place, arrays, results, apart=outs, out_hbm=True,
                scratch=[pltpu.VMEM((width, cols), f32), pltpu.VMEM((width, cols), bf16),
                         pltpu.VMEM((width, cols), bf16),
                         pltpu.SemaphoreType.DMA((3, width // TILE))],
                limit=16, flops=2 * rows * width * cols, aliases=aliases)


def delta_for_core(place, delta):
    rows, cols = delta.shape
    part = rows // REP

    def body(place, delta_ref, out_ref):
        for j in range(REP // 2):
            source = pl.ds(pl.multiple_of((2 * j + 1 - place[4]) * part, part), part)
            out_ref[j * part : (j + 1) * part, :] = delta_ref[source, :].astype(bf16)

    return call(body, "delta_for_core", place, [delta], [((rows // 2, cols), bf16)])[0]


def delta_for_ring(place, delta, got):
    rows, cols = delta.shape
    part = rows // REP

    def body(place, delta_ref, got_ref, own_ref, s1, s2, s3):
        for hops in range(RING):
            ring = lax.rem(place[2] + hops, RING)
            for far in range(2):
                j = 2 * ring + far
                near = pl.ds(pl.multiple_of((2 * j + place[4]) * part, part), part)
                sent = pl.ds(pl.multiple_of(j * part, part), part)
                total = delta_ref[near, :] + got_ref[sent, :].astype(f32)
                block = slice(far * part, (far + 1) * part)
                if hops:
                    (s1, s2, s3)[hops - 1][block, :] = total.astype(bf16)
                else:
                    own_ref[block, :] = total

    return call(body, "delta_for_ring", place, [delta, got],
                [((2 * part, cols), f32)] + [((2 * part, cols), bf16)] * (RING - 1))


def delta_for_far(place, own, got, anchor, momentum):
    rows, cols = own.shape
    part = anchor.shape[2]

    def body(place, own_ref, g1, g2, g3, a_ref, p_ref, keep_ref, send_ref):
        total = own_ref[...]
        for ref in (g1, g2, g3):
            total = total + ref[...].astype(f32)
        keep_ref[...] = total
        send_ref[:rows, :] = total.astype(bf16)
        base = a_ref[place[5], 0] - outer_rate * outer_mu * outer_mu * p_ref[place[5], 0]
        send_ref[rows:, :] = base.astype(bf16)

    return call(body, "delta_for_far", place, [own, *got, anchor, momentum],
                [(own.shape, f32), ((rows + part, cols), bf16)])


def outer_step(place, keep, got, anchor, momentum):
    _, _, part, cols = anchor.shape

    def body(place, keep_ref, got_ref, a_ref, p_ref, a_out, p_out, new_ref):
        a_out[...] = a_ref[...]
        p_out[...] = p_ref[...]
        fragment = place[5]
        for far in range(2):
            block = slice(far * part, (far + 1) * part)
            mean = (keep_ref[block, :] + got_ref[block, :].astype(f32)) / REP

            @pl.when(place[3] == far)
            def _():
                moment = outer_mu * p_ref[fragment, 0] + mean
                fresh = a_ref[fragment, 0] - outer_rate * (mean + outer_mu * moment)
                p_out[fragment, 0] = moment
                a_out[fragment, 0] = fresh
                new_ref[block, :] = fresh.astype(bf16)

            @pl.when(place[3] != far)
            def _():
                base = got_ref[2 * part :, :].astype(f32)
                fresh = base - outer_rate * (1.0 + outer_mu) * mean
                new_ref[block, :] = fresh.astype(bf16)

    return call(body, "outer_step", place, [keep, got, anchor, momentum],
                [(anchor.shape, f32), (momentum.shape, f32), (keep.shape, bf16)])


def join_ring(place, pieces):
    part, cols = pieces[0].shape

    def body(place, p0, p1, p2, p3, out_ref):
        for hops, ref in enumerate((p0, p1, p2, p3)):
            out_ref[ring_rows(place[2], RING - hops, part), :] = ref[...]

    return call(body, "join_ring", place, pieces, [((RING * part, cols), bf16)])[0]


class InOrder:
    def __init__(self, place):
        self.place = place

    def __call__(self, kernel, *args):
        results = kernel(self.place, *args)
        single = not isinstance(results, (list, tuple))
        results = [results] if single else list(results)
        results[-1] = self.after(results[-1])
        return results[0] if single else results

    def after(self, value):
        self.place, value = lax.optimization_barrier((self.place, value))
        return value


def by_hops(values):
    return [shift_y(values[hops - 1], hops) for hops in (1, 2, 3)]


def resids_of(run, modes, parts, targets, step, chain, inv_root):
    reduce_mode, gather_mode = modes
    own, *sent = parts
    if reduce_mode == "x":
        own, *sent = run(add_far_keys, own, swap_x(sent[0]))
        got = by_hops(sent)
        yield
        resid = run(sum_keys, own, got, targets, step, chain, inv_root)
        if gather_mode == "x":
            resids = [resid, *by_hops([resid] * 3)]
            yield
            yield [*resids, swap_x(run(join_resids, resids))]
            return
        other = swap_x(resid)
        yield
        resid = run(join_pair, resid, other)
    else:
        k1, k2, k3 = sent
        if reduce_mode == "direct":
            got = by_hops(sent)
        elif reduce_mode == "up":
            relay = run(add_keys, k1, shift_y(k2, 1))
            got = [shift_y(relay, 1), shift_y(k3, 3)]
            yield
        else:
            relay = run(add_keys, k3, shift_y(k2, 3))
            got = [shift_y(relay, 3), shift_y(k1, 1)]
            yield
        half = run(sum_keys, own, got, targets, step, chain, inv_root)
        other = swap_x(half)
        yield
        resid = run(pair_resid, half, other)
    if gather_mode == "direct":
        resids = [resid, *by_hops([resid] * 3)]
    else:
        up, down = shift_y(resid, 1), shift_y(resid, 3)
        resids = [resid, up, shift_y(up, 1) if gather_mode == "up" else shift_y(down, 3), down]
    yield resids


def on_device(tokens, targets, params, moment1, moment2, stale_delta, anchor, momentum, plan):
    inv_root = 1.0 / math.sqrt(tokens.shape[3])
    here = lax.axis_index("fsdp")
    home = lax.axis_index("rep")
    run = InOrder(
        jnp.stack(
            [here >> 1, here & 1, home >> 2, (home >> 1) & 1, home & 1, plan[0]]
        ).astype(jnp.int32)
    )
    cols = stale_delta.shape[2]
    chains = range(params.shape[2] // cols)
    delta = stale_delta[0]

    toks = run.after(regroup_tokens(tokens, 0))
    toks = lax.all_to_all(toks, "fsdp", split_axis=0, concat_axis=0, tiled=True)
    toks = toks.reshape(-1, toks.shape[-1])

    up, down, far, near, opposite = run(tokens_by_hops, tokens, 1)
    up, down, far = shift_y(up, 1), shift_y(down, 3), swap_x(far)
    got = swap_core(run(delta_for_core, delta))
    own, *sent = run(delta_for_ring, delta, got)
    got = [shift_z(sent[h - 1], h) for h in (1, 2, 3)]
    narrow = run(narrow_chains, params, cols)
    keep, send = run(delta_for_far, own, got, anchor, momentum)
    toks = run.after(toks)

    parts = {}
    for chain in chains:
        parts[chain] = run(first_keys, MODES[0][chain][0], toks, narrow[chain])
    steps = [resids_of(run, MODES[0][c], parts[c], targets, 0, c, inv_root) for c in chains]
    resids = {}

    def advance(order):
        nonlocal got, fresh, anchors, next_toks, opposite, sides, far
        for name in order:
            if name in ("A", "B"):
                chain = ("A", "B").index(name)
                resids[chain] = next(steps[chain])
            elif name == "pairs":
                opposite = shift_y(run(join_blocks, opposite, 0, far, 1), 2)
            elif name == "far":
                far = run.after(far)
            elif name == "sides":
                sides = swap_x(run(join_blocks, up, 1, down, 1))
            elif name == "join":
                next_toks = run.after([near, far, up, down, opposite, sides])
            elif name == "outer":
                results.extend(run(outer_step, keep, swap_far(send), anchor, momentum))
                fresh = results.pop()
                up_z, down_z = shift_z(fresh, 1), shift_z(fresh, 3)
                got = [up_z, shift_z(up_z, 1), down_z]
            elif name == "ring":
                fresh = run(join_ring, [fresh, *got])
                anchors = (fresh, swap_core(fresh))

    results = []
    fresh = anchors = next_toks = sides = None
    advance(ORDER[0])
    state = {}
    for chain in chains:
        w, m, v, *parts[chain] = run(
            middle_step, MODES[1][chain][0], toks, next_toks, resids[chain], params, moment1,
            moment2, chain, inv_root
        )
        state[chain] = (w, m, v)
    steps = [resids_of(run, MODES[1][c], parts[c], targets, 1, c, inv_root) for c in chains]
    advance(ORDER[1])
    outs = []
    for chain in chains:
        outs = run(last_step, next_toks, resids[chain], *state[chain], anchors, chain, inv_root, outs)
    return (*outs, *results)


def solution(mesh):
    return jax.shard_map(
        on_device,
        mesh=mesh,
        in_specs=(
            P("rep", None, "fsdp", None),
            P("rep", None, "fsdp", None),
            P("rep", "fsdp", None),
            P("rep", "fsdp", None),
            P("rep", "fsdp", None),
            P("rep", "fsdp", None),
            P(None, "fsdp", "rep", None),
            P(None, "fsdp", "rep", None),
            P(),
        ),
        out_specs=(
            P("rep", "fsdp", None),
            P("rep", "fsdp", None),
            P("rep", "fsdp", None),
            P(None, "fsdp", "rep", None),
            P(None, "fsdp", "rep", None),
        ),
        check_vma=False,
    )
```
